512 devices in a mesh: ctx: 64 (over y, z_lo, core), head: 8 (over z_hi, x).
Axes of the slice: x: 4, y: 8, z: 8 (z_hi: 2, z_lo: 4; z = z_hi * 4 + z_lo), core: 2. Of those that a mesh axis runs over, the one named last changes fastest.
Arguments:
- queries: bfloat16 [8192, 2048], P('ctx', 'head'), may hold values from -6 to 6
- keys: bfloat16 [8192, 2048], P('ctx', 'head'), may hold values from -6 to 6
- values: bfloat16 [8192, 2048], P('ctx', 'head'), may hold values from -6 to 6
- out_grad: bfloat16 [8192, 2048], P(('ctx', 'head')), may hold values from -6 to 6
Outputs:
- query_grad: bfloat16 [8192, 2048], P('ctx', 'head')
- key_grad: bfloat16 [8192, 2048], P('ctx', 'head')
- value_grad: bfloat16 [8192, 2048], P('ctx', 'head')
The draws below stay inside these ranges and needn't reach their ends.
All inputs are finite; a program needn't handle non-finite values.
Results may differ from the reference program's by a relative error of at most 0.01.
Values may be sent and summed in bfloat16 or wider, within the bound.
No kernel may reach another device: no remote copies, remote signals or barrier semaphores. Data moves between devices by JAX's collectives and lax.ppermute only.
A program may use at most 64 MiB of HBM per device.

```python
import jax
import jax.numpy as jnp
from jax import lax

D_HEAD = 64
WIDTH = 2048
SEQ = 8192


def draw_queries(key, part):
    key = jax.random.fold_in(key, 7)
    result = jnp.clip(jax.random.normal(key, (SEQ, WIDTH)), -5.0, 5.0)
    return result.astype(jnp.bfloat16)


def draw_keys(key, part):
    key = jax.random.fold_in(key, 8)
    result = jnp.clip(jax.random.normal(key, (SEQ, WIDTH)), -5.0, 5.0)
    return result.astype(jnp.bfloat16)


def block_levels(own_key, dims, pieces, smallest, largest):
    factor_of, own = 1.0, jax.random.fold_in(own_key, 6)
    for axis_at, parts in pieces:
        heights = jnp.exp(jax.random.uniform(jax.random.fold_in(own, axis_at), (parts,), jnp.float32, smallest / len(pieces), largest / len(pieces)))
        factor_of = factor_of * jnp.repeat(heights, dims[axis_at] // parts).reshape([-1 if axis == axis_at else 1 for axis in range(len(dims))])
    return factor_of


def bell_draw(key, dims, scale, limit, shards=(), kind=jnp.bfloat16):
    factor_of = block_levels(key, dims, shards, -0.22, 0.18) if shards else 1.0
    values = jax.random.normal(key, dims, jnp.float32) * scale * factor_of
    return jnp.minimum(jnp.maximum(values, -limit), limit).astype(kind)


def setup_inputs(seed: int = 0) -> dict:
    key_list = jax.random.split(jax.random.key(seed), 5)
    return {
        "queries": draw_queries(jax.random.fold_in(key_list[4], 71), 0),
        "keys": draw_keys(jax.random.fold_in(key_list[4], 71), 0),
        "values": bell_draw(key_list[2], (SEQ, WIDTH), 1.0, 6.0, ((0, 64), (1, 8))),
        "out_grad": bell_draw(key_list[3], (SEQ, WIDTH), 1.0, 6.0, ((0, 512),)),
    }


neg_fill = -1.0e30


def reference(queries, keys, values, out_grad):
    seq_len = queries.shape[0]
    width = queries.shape[1]
    num_heads = width // D_HEAD
    scale = D_HEAD ** -0.5
    query_heads = queries.reshape(seq_len, num_heads, D_HEAD).astype(jnp.float32)
    key_heads = keys.reshape(seq_len, num_heads, D_HEAD).astype(jnp.float32)
    value_heads = values.reshape(seq_len, num_heads, D_HEAD).astype(jnp.float32)
    grad_heads = out_grad.reshape(seq_len, num_heads, D_HEAD).astype(jnp.float32)
    block = min(256, seq_len)
    key_total = jnp.zeros((seq_len, num_heads, D_HEAD), jnp.float32)
    value_total = jnp.zeros((seq_len, num_heads, D_HEAD), jnp.float32)
    query_pieces = []
    for block_index in range(seq_len // block):
        row_start = block_index * block
        row_end = row_start + block
        query_block = query_heads[row_start:row_end]
        grad_block = grad_heads[row_start:row_end]
        key_block = key_heads[:row_end]
        value_block = value_heads[:row_end]
        scores = jnp.einsum("qhd,khd->hqk", query_block, key_block) * scale
        query_pos = row_start + jnp.arange(block)
        key_pos = jnp.arange(row_end)
        allowed = key_pos[None, :] <= query_pos[:, None]
        scores = jnp.where(allowed[None], scores, neg_fill)
        top = jnp.max(scores, axis=2, keepdims=True)
        log_total = top + jnp.log(jnp.sum(jnp.exp(scores - top), axis=2, keepdims=True))
        probs = jnp.exp(scores - log_total)
        probs_low = lax.optimization_barrier(probs.astype(jnp.bfloat16)).astype(jnp.float32)
        attn_out = jnp.einsum("hqk,khd->qhd", probs_low, value_block)
        delta = jnp.sum(grad_block * attn_out, axis=2)
        dprobs = jnp.einsum("qhd,khd->hqk", grad_block, value_block)
        dscores = probs * (dprobs - delta.T[:, :, None])
        dscores = lax.optimization_barrier(dscores.astype(jnp.bfloat16)).astype(jnp.float32)
        query_pieces.append(jnp.einsum("hqk,khd->qhd", dscores, key_block) * scale)
        key_total = key_total.at[:row_end].add(jnp.einsum("hqk,qhd->khd", dscores, query_block) * scale)
        value_total = value_total.at[:row_end].add(jnp.einsum("hqk,qhd->khd", probs_low, grad_block))
    query_total = jnp.concatenate(query_pieces, axis=0)
    return (query_total.reshape(seq_len, width).astype(jnp.bfloat16),
            key_total.reshape(seq_len, width).astype(jnp.bfloat16),
            value_total.reshape(seq_len, width).astype(jnp.bfloat16))
```

```python
import functools

import jax
import jax.numpy as jnp
from jax import lax
from jax.experimental import pallas as pl
from jax.experimental.pallas import tpu as pltpu
from jax.sharding import Mesh
from jax.sharding import PartitionSpec as P

D_HEAD = 64
TOK = 128
GROUP = 4
SIDE = TOK * GROUP
SCALE = D_HEAD ** (-0.5)
EXP2_SCALE = SCALE * 1.4426950408889634
NEG = -1e30
FLOPS_PER_MICRO = 10**9
BF = jnp.bfloat16
F32 = jnp.float32

PART = TOK // GROUP
CHIPS = 32
HEADS = 8
PER = SIDE // PART // 2
HALF = SIDE // 2
QUAD = PER // 2
FULL = GROUP * (GROUP - 1) // 2


def chip_of(b, r1, c):
    return b * 8 + (c // 2) * 4 + r1 * 2 + c % 2


def call(body, out_shapes, scratch, *operands, micros=1, space=pltpu.VMEM, vmem=24):
    spaces = [pltpu.SMEM if x.dtype == jnp.int32 else space for x in operands]
    return pl.pallas_call(
        body,
        out_shape=out_shapes,
        in_specs=[pl.BlockSpec(memory_space=space) for space in spaces],
        out_specs=jax.tree.map(lambda _: pl.BlockSpec(memory_space=pltpu.VMEM), out_shapes),
        scratch_shapes=scratch,
        cost_estimate=pl.CostEstimate(
            flops=micros * FLOPS_PER_MICRO, bytes_accessed=2**20, transcendentals=0
        ),
        compiler_params=pltpu.CompilerParams(vmem_limit_bytes=vmem * 2**20),
    )(*operands)


def shape(*dims, dtype=BF):
    return jax.ShapeDtypeStruct(dims, dtype)


def split_grad(grad, out_ref):
    for g in range(HEADS):
        out_ref[g] = grad[:, g * GROUP * D_HEAD : (g + 1) * GROUP * D_HEAD]


def pack_body(at, q_ref, k_ref, v_ref, g_ref, out_ref, stage):
    core = at[2]
    for b in range(GROUP):
        lanes = slice(b * D_HEAD, (b + 1) * D_HEAD)
        both = jnp.concatenate([k_ref[:, lanes], v_ref[:, lanes]], axis=1)
        rows = jnp.concatenate([q_ref[:, lanes], g_ref[:, lanes]], axis=1)
        stage[...] = rows.reshape(GROUP, PART, 2 * D_HEAD)
        for r1 in range(2):
            keep, give = stage[2 * r1 + core], stage[2 * r1 + 1 - core]
            for c in range(GROUP):
                to = chip_of(b, r1, c)
                out_ref[to, :PART, :] = keep
                out_ref[to, PART : 2 * PART, :] = both[c * PART : (c + 1) * PART, :]
                out_ref[to, 2 * PART :, :] = give


def give_body(data, give_ref):
    give_ref[...] = data[:, PART:, :]


def make_bias(at):
    r, c, core = at[0], at[1], at[2]

    def block_start(index):
        block = 2 * ((index // PART) % QUAD) + (core ^ index // (HALF // 2))
        return block * TOK + index % PART

    key_pos = block_start(lax.broadcasted_iota(jnp.int32, (HALF, 1), 0)) + c * PART
    query_pos = block_start(lax.broadcasted_iota(jnp.int32, (1, HALF), 1)) + r * PART
    return jnp.where(key_pos <= query_pos, 0.0, NEG)


def mm(a, b):
    return lax.dot_general(a, b, (((1,), (0,)), ((), ())), preferred_element_type=F32)


def blocks(own, other, at):
    return jnp.concatenate(
        [
            ref[at * PER + half * QUAD : at * PER + (half + 1) * QUAD, first : first + PART, :]
            .reshape(HALF // 2, 2 * D_HEAD)
            for half in range(2)
            for ref, first in (own, other)
        ],
        axis=0,
    )


def row_block(data, other, u):
    return blocks((data, 0), (other, PART), u)


def col_block(data, other, v):
    return blocks((data, PART), (other, 0), v)


def below(v, u):
    return u * (u - 1) // 2 + v


def halves(both, axis):
    first = lax.broadcasted_iota(jnp.int32, both.shape, axis) < D_HEAD
    zeros = jnp.zeros_like(both)
    return jnp.where(first, both, zeros), jnp.where(first, zeros, both)


def stats_body(at, data, other, out_ref, *saved):
    s_tiles, dp_tiles = saved[:3], saved[3:]
    bias = make_bias(at)

    def multiply(u):
        q_low, g_low = halves(row_block(data, other, u).T, 0)
        kv_low = col_block(data, other, u)
        s = mm(kv_low[:HALF], q_low) * EXP2_SCALE
        s = jnp.concatenate([s[:, :HALF] + bias, s[:, HALF:]], axis=1)
        s_tiles[1][u] = s
        dp_tiles[1][u] = mm(kv_low[:HALF], g_low)
        top = jnp.max(s, axis=0, keepdims=True)
        yield None
        late = mm(kv_low[HALF:], q_low[:, HALF:]) * EXP2_SCALE + bias
        s_tiles[2][u] = late
        dp_tiles[2][u] = mm(kv_low[HALF:], g_low[:, HALF:])
        late_top = jnp.max(late, axis=0, keepdims=True)
        top = jnp.concatenate([top[:, :HALF], jnp.maximum(top[:, HALF:], late_top)], axis=1)
        yield top
        for v in range(u):
            kv_low = col_block(data, other, v)
            s = mm(kv_low, q_low) * EXP2_SCALE
            s_tiles[0][below(v, u)] = s
            dp_tiles[0][below(v, u)] = mm(kv_low, g_low)
            top = jnp.maximum(top, jnp.max(s, axis=0, keepdims=True))
            yield top

    def add_up(u, top):
        def sums(s, dp, top):
            p = jnp.exp2(s - top)
            return jnp.sum(p, axis=0, keepdims=True), jnp.sum(p * dp, axis=0, keepdims=True)

        first = sums(s_tiles[1][u], dp_tiles[1][u], top)
        yield None
        late = sums(s_tiles[2][u], dp_tiles[2][u], top[:, HALF:])
        total, weighted = (
            jnp.concatenate([a[:, :HALF], a[:, HALF:] + b], axis=1) for a, b in zip(first, late)
        )
        for v in range(u):
            yield None
            more = sums(s_tiles[0][below(v, u)], dp_tiles[0][below(v, u)], top)
            total, weighted = total + more[0], weighted + more[1]
        for d in range(GROUP):
            out_ref[d, u : u + 1, :] = top + jnp.log2(total)
            out_ref[d, u + GROUP : u + GROUP + 1, :] = weighted / total

    behind = iter(())
    for u in reversed(range(GROUP)):
        for top in multiply(u):
            next(behind, None)
        for _ in behind:
            pass
        behind = add_up(u, top)
    for _ in behind:
        pass


def grads_body(data, other, stats, *rest):
    s_tiles, dp_tiles, (dkv_ref, dq_ref, give_ref) = rest[:3], rest[3:6], rest[6:9]
    row_ref, q_rows, g_rows, dq_acc, dkv_acc = rest[9:]
    logs = [stats[d, :GROUP, :] for d in range(GROUP)]
    top = functools.reduce(jnp.maximum, logs)
    weights = [jnp.exp2(one - top) for one in logs]
    total = sum(weights)
    row_ref[:GROUP, :] = top + jnp.log2(total)
    row_ref[GROUP:, :] = sum(w * stats[d, GROUP:, :] for d, w in enumerate(weights)) / total
    for u in range(GROUP):
        q_rows[u], g_rows[u] = halves(row_block(data, other, u), 1)

    def probs_of(s, dp, u, lanes):
        p = jnp.exp2(s - row_ref[u : u + 1, lanes])
        ds = p * (dp - row_ref[GROUP + u : GROUP + u + 1, lanes])
        return p.astype(BF), ds.astype(BF)

    def both_grads(p, ds, u, lanes):
        return mm(ds, q_rows[u, lanes, :]) + mm(p, g_rows[u, lanes, :])

    late_lanes, lane = slice(HALF, SIDE), lax.broadcasted_iota(jnp.int32, (1, TOK), 1)
    factor = jnp.where(lane < D_HEAD, SCALE, 1.0)
    for v in range(GROUP):
        k_t = col_block(data, other, v).T[:D_HEAD, :]
        p, ds = probs_of(s_tiles[1][v], dp_tiles[1][v], v, slice(0, SIDE))
        dkv_acc[:HALF] = both_grads(p, ds, v, slice(0, SIDE))
        dq = mm(k_t[:, :HALF], ds)
        p, ds = probs_of(s_tiles[2][v], dp_tiles[2][v], v, late_lanes)
        dkv_acc[HALF:] = both_grads(p, ds, v, late_lanes)
        dq = jnp.concatenate([dq[:, :HALF], dq[:, HALF:] + mm(k_t[:, HALF:], ds)], axis=1)
        dq_acc[v] = dq if v == 0 else dq_acc[v] + dq
        for u in range(v + 1, GROUP):
            p, ds = probs_of(s_tiles[0][below(v, u)], dp_tiles[0][below(v, u)], u, slice(0, SIDE))
            dq = mm(k_t, ds)
            dq_acc[u] = dq if v == 0 else dq_acc[u] + dq
            dkv_acc[...] += both_grads(p, ds, u, slice(0, SIDE))
        done = (dkv_acc[...] * factor).astype(BF).reshape(2, 2, QUAD, PART, 2 * D_HEAD)
        for half in range(2):
            chips = slice(v * PER + half * QUAD, v * PER + (half + 1) * QUAD)
            dkv_ref[chips] = done[half, 0]
            give_ref[chips, :PART, :] = done[half, 1]
    for u in range(GROUP):
        dq = (dq_acc[u] * SCALE).T.astype(BF).reshape(2, 2, QUAD, PART, D_HEAD)
        dq = jnp.concatenate([dq[..., : PART // 2, :], dq[..., PART // 2 :, :]], axis=4)
        for half in range(2):
            chips = slice(u * PER + half * QUAD, u * PER + (half + 1) * QUAD)
            dq_ref[chips] = dq[half, 0]
            give_ref[chips, PART:, :] = dq[half, 1]


def pair_body(at, dkv, dq, got, out_ref):
    core = at[2]
    half = PART // 2
    out_ref[:, :PART, :] = (dkv[...].astype(F32) + got[:, :PART, :].astype(F32)).astype(BF)
    out_ref[:, pl.ds(pl.multiple_of(PART + core * half, half), half), :] = dq[...]
    out_ref[:, pl.ds(pl.multiple_of(PART + (1 - core) * half, half), half), :] = got[:, PART:, :]


def sum_body(part, dq_ref, dk_ref, dv_ref):
    def cols_of(b, c):
        return sum(part[chip_of(b, r1, c), :PART, :].astype(F32) for r1 in range(2))

    def rows_of(b, r):
        lines = slice(PART + (r % 2) * (PART // 2), PART + (r % 2 + 1) * (PART // 2))
        both = sum(part[chip_of(b, r // 2, c), lines, :].astype(F32) for c in range(GROUP))
        return jnp.concatenate([both[:, :D_HEAD], both[:, D_HEAD:]], axis=0)

    for pair in range(2):
        lanes = slice(pair * 2 * D_HEAD, (pair + 1) * 2 * D_HEAD)
        heads = (2 * pair, 2 * pair + 1)
        for x in range(GROUP):
            toks = slice(x * PART, (x + 1) * PART)
            dkv = [cols_of(b, x) for b in heads]
            dq_ref[toks, lanes] = jnp.concatenate([rows_of(b, x) for b in heads], axis=1).astype(BF)
            dk_ref[toks, lanes] = jnp.concatenate([a[:, :D_HEAD] for a in dkv], axis=1).astype(BF)
            dv_ref[toks, lanes] = jnp.concatenate([a[:, D_HEAD:] for a in dkv], axis=1).astype(BF)


CHIP_AXES = ("b", "c1", "r1", "c0")


def swap(piece, axes):
    return lax.all_to_all(piece, axes, split_axis=0, concat_axis=0, tiled=True)


def meet(piece):
    return lax.ppermute(piece, "core", [(0, 1), (1, 0)])


def shards(queries, keys, values, out_grad):
    core = lax.axis_index("core")
    r = 2 * lax.axis_index("r1") + core
    c = 2 * lax.axis_index("c1") + lax.axis_index("c0")
    at = jnp.stack([r, c, core]).astype(jnp.int32)
    wide = GROUP * D_HEAD
    grad_parts = call(split_grad, shape(HEADS, TOK // HEADS, wide), [], out_grad)
    grad_local = swap(grad_parts, "head").reshape(TOK, wide)
    data = swap(
        call(
            pack_body,
            shape(CHIPS, 3 * PART, 2 * D_HEAD),
            [pltpu.VMEM((GROUP, PART, 2 * D_HEAD), BF)],
            at, queries, keys, values, grad_local,
        ),
        CHIP_AXES,
    )
    other = meet(call(give_body, shape(CHIPS, 2 * PART, 2 * D_HEAD), [], data))
    stat = shape(GROUP, 2 * GROUP, SIDE, dtype=F32)
    tiles = [
        shape(FULL, SIDE, SIDE, dtype=F32),
        shape(GROUP, HALF, SIDE, dtype=F32),
        shape(GROUP, HALF, HALF, dtype=F32),
    ]
    stats, *saved = call(stats_body, [stat, *tiles, *tiles], [], at, data, other, micros=5)
    stats = swap(stats, ("c1", "c0"))
    half = PART // 2
    dkv, dq, give = call(
        grads_body,
        [
            shape(CHIPS, PART, 2 * D_HEAD),
            shape(CHIPS, half, 2 * D_HEAD),
            shape(CHIPS, PART + half, 2 * D_HEAD),
        ],
        [
            pltpu.VMEM(stat.shape[1:], F32),
            pltpu.VMEM((GROUP, SIDE, 2 * D_HEAD), BF),
            pltpu.VMEM((GROUP, SIDE, 2 * D_HEAD), BF),
            pltpu.VMEM((GROUP, D_HEAD, SIDE), F32),
            pltpu.VMEM((SIDE, 2 * D_HEAD), F32),
        ],
        data, other, stats, *saved,
        micros=7,
    )
    partial = call(
        pair_body, shape(CHIPS, 2 * PART, 2 * D_HEAD), [], at, dkv, dq, meet(give)
    )
    return tuple(call(sum_body, [shape(TOK, wide)] * 3, [], swap(partial, CHIP_AXES)))


def solution(mesh):
    ctx = (*CHIP_AXES, "core")
    split = Mesh(mesh.devices.reshape(4, 2, 2, 2, 2, HEADS), (*ctx, "head"))
    placed = (P(ctx, "head"), P(ctx, "head"), P(ctx, "head"), P((*ctx, "head"), None))
    return jax.shard_map(
        shards,
        mesh=split,
        in_specs=placed,
        out_specs=placed[:3],
        check_vma=False,
    )
```

```python
import functools

import jax
import jax.numpy as jnp
from jax import lax
from jax.experimental import pallas as pl
from jax.experimental.pallas import tpu as pltpu
from jax.sharding import Mesh
from jax.sharding import PartitionSpec as P

D_HEAD = 64
TOK = 128
GROUP = 4
SIDE = TOK * GROUP
SCALE = D_HEAD ** (-0.5)
EXP2_SCALE = SCALE * 1.4426950408889634
NEG = -1e30
FLOPS_PER_MICRO = 10**9
BF = jnp.bfloat16
F32 = jnp.float32

PART = TOK // GROUP
CHIPS = 32
HEADS = 8
PER = SIDE // PART // 2
HALF = SIDE // 2
QUAD = PER // 2
FULL = GROUP * (GROUP - 1) // 2


def chip_of(b, r1, c):
    return b * 8 + (c // 2) * 4 + r1 * 2 + c % 2


def call(body, out_shapes, scratch, *operands, micros=1, space=pltpu.VMEM, vmem=24):
    spaces = [pltpu.SMEM if x.dtype == jnp.int32 else space for x in operands]
    return pl.pallas_call(
        body,
        out_shape=out_shapes,
        in_specs=[pl.BlockSpec(memory_space=space) for space in spaces],
        out_specs=jax.tree.map(lambda _: pl.BlockSpec(memory_space=pltpu.VMEM), out_shapes),
        scratch_shapes=scratch,
        cost_estimate=pl.CostEstimate(
            flops=micros * FLOPS_PER_MICRO, bytes_accessed=2**20, transcendentals=0
        ),
        compiler_params=pltpu.CompilerParams(vmem_limit_bytes=vmem * 2**20),
    )(*operands)


def shape(*dims, dtype=BF):
    return jax.ShapeDtypeStruct(dims, dtype)


def split_grad(grad, out_ref):
    for g in range(HEADS):
        out_ref[g] = grad[:, g * GROUP * D_HEAD : (g + 1) * GROUP * D_HEAD]


def pack_body(at, q_ref, k_ref, v_ref, out_ref, stage):
    core = at[2]
    for b in range(GROUP):
        lanes = slice(b * D_HEAD, (b + 1) * D_HEAD)
        both = jnp.concatenate([k_ref[:, lanes], v_ref[:, lanes]], axis=1)
        rows = jnp.concatenate([q_ref[:, lanes], q_ref[:, lanes]], axis=1)
        stage[...] = rows.reshape(GROUP, PART, 2 * D_HEAD)
        for r1 in range(2):
            keep, give = stage[2 * r1 + core], stage[2 * r1 + 1 - core]
            for c in range(GROUP):
                to = chip_of(b, r1, c)
                out_ref[to, :PART, :] = keep
                out_ref[to, PART : 2 * PART, :] = both[c * PART : (c + 1) * PART, :]
                out_ref[to, 2 * PART :, :] = give


def add_grad(at, g_ref, part_ref, out_ref, stage):
    core = at[2]
    first = lax.broadcasted_iota(jnp.int32, (PART, 2 * D_HEAD), 1) < D_HEAD
    for b in range(GROUP):
        lanes = slice(b * D_HEAD, (b + 1) * D_HEAD)
        rows = jnp.concatenate([g_ref[:, lanes], g_ref[:, lanes]], axis=1)
        stage[...] = rows.reshape(GROUP, PART, 2 * D_HEAD)
        for r1 in range(2):
            keep, give = stage[2 * r1 + core], stage[2 * r1 + 1 - core]
            for c in range(GROUP):
                to = chip_of(b, r1, c)
                out_ref[to, :PART, :] = jnp.where(first, part_ref[to, :PART, :], keep)
                out_ref[to, PART : 2 * PART, :] = part_ref[to, PART : 2 * PART, :]
                out_ref[to, 2 * PART :, :] = jnp.where(first, part_ref[to, 2 * PART :, :], give)


def give_body(data, give_ref):
    give_ref[...] = data[:, PART:, :]


def make_bias(at):
    r, c, core = at[0], at[1], at[2]

    def block_start(index):
        block = 2 * ((index // PART) % QUAD) + (core ^ index // (HALF // 2))
        return block * TOK + index % PART

    key_pos = block_start(lax.broadcasted_iota(jnp.int32, (HALF, 1), 0)) + c * PART
    query_pos = block_start(lax.broadcasted_iota(jnp.int32, (1, HALF), 1)) + r * PART
    return jnp.where(key_pos <= query_pos, 0.0, NEG)


def mm(a, b):
    return lax.dot_general(a, b, (((1,), (0,)), ((), ())), preferred_element_type=F32)


def blocks(own, other, at):
    return jnp.concatenate(
        [
            ref[at * PER + half * QUAD : at * PER + (half + 1) * QUAD, first : first + PART, :]
            .reshape(HALF // 2, 2 * D_HEAD)
            for half in range(2)
            for ref, first in (own, other)
        ],
        axis=0,
    )


def row_block(data, other, u):
    return blocks((data, 0), (other, PART), u)


def col_block(data, other, v):
    return blocks((data, PART), (other, 0), v)


def below(v, u):
    return u * (u - 1) // 2 + v


def halves(both, axis):
    first = lax.broadcasted_iota(jnp.int32, both.shape, axis) < D_HEAD
    zeros = jnp.zeros_like(both)
    return jnp.where(first, both, zeros), jnp.where(first, zeros, both)


def stats_body(at, data, other, out_ref, *saved):
    s_tiles, dp_tiles = saved[:3], saved[3:]
    bias = make_bias(at)

    def multiply(u):
        q_low, g_low = halves(row_block(data, other, u).T, 0)
        kv_low = col_block(data, other, u)
        s = mm(kv_low[:HALF], q_low) * EXP2_SCALE
        s = jnp.concatenate([s[:, :HALF] + bias, s[:, HALF:]], axis=1)
        s_tiles[1][u] = s
        dp_tiles[1][u] = mm(kv_low[:HALF], g_low)
        top = jnp.max(s, axis=0, keepdims=True)
        yield None
        late = mm(kv_low[HALF:], q_low[:, HALF:]) * EXP2_SCALE + bias
        s_tiles[2][u] = late
        dp_tiles[2][u] = mm(kv_low[HALF:], g_low[:, HALF:])
        late_top = jnp.max(late, axis=0, keepdims=True)
        top = jnp.concatenate([top[:, :HALF], jnp.maximum(top[:, HALF:], late_top)], axis=1)
        yield top
        for v in range(u):
            kv_low = col_block(data, other, v)
            s = mm(kv_low, q_low) * EXP2_SCALE
            s_tiles[0][below(v, u)] = s
            dp_tiles[0][below(v, u)] = mm(kv_low, g_low)
            top = jnp.maximum(top, jnp.max(s, axis=0, keepdims=True))
            yield top

    def add_up(u, top):
        def sums(s, dp, top):
            p = jnp.exp2(s - top)
            return jnp.sum(p, axis=0, keepdims=True), jnp.sum(p * dp, axis=0, keepdims=True)

        first = sums(s_tiles[1][u], dp_tiles[1][u], top)
        yield None
        late = sums(s_tiles[2][u], dp_tiles[2][u], top[:, HALF:])
        total, weighted = (
            jnp.concatenate([a[:, :HALF], a[:, HALF:] + b], axis=1) for a, b in zip(first, late)
        )
        for v in range(u):
            yield None
            more = sums(s_tiles[0][below(v, u)], dp_tiles[0][below(v, u)], top)
            total, weighted = total + more[0], weighted + more[1]
        for d in range(GROUP):
            out_ref[d, u : u + 1, :] = top + jnp.log2(total)
            out_ref[d, u + GROUP : u + GROUP + 1, :] = weighted / total

    behind = iter(())
    for u in reversed(range(GROUP)):
        for top in multiply(u):
            next(behind, None)
        for _ in behind:
            pass
        behind = add_up(u, top)
    for _ in behind:
        pass


def grads_body(data, other, stats, *rest):
    s_tiles, dp_tiles, (dkv_ref, dq_ref, give_ref) = rest[:3], rest[3:6], rest[6:9]
    row_ref, q_rows, g_rows, dq_acc, dkv_acc = rest[9:]
    logs = [stats[d, :GROUP, :] for d in range(GROUP)]
    top = functools.reduce(jnp.maximum, logs)
    weights = [jnp.exp2(one - top) for one in logs]
    total = sum(weights)
    row_ref[:GROUP, :] = top + jnp.log2(total)
    row_ref[GROUP:, :] = sum(w * stats[d, GROUP:, :] for d, w in enumerate(weights)) / total
    for u in range(GROUP):
        q_rows[u], g_rows[u] = halves(row_block(data, other, u), 1)

    def probs_of(s, dp, u, lanes):
        p = jnp.exp2(s - row_ref[u : u + 1, lanes])
        ds = p * (dp - row_ref[GROUP + u : GROUP + u + 1, lanes])
        return p.astype(BF), ds.astype(BF)

    def both_grads(p, ds, u, lanes):
        return mm(ds, q_rows[u, lanes, :]) + mm(p, g_rows[u, lanes, :])

    late_lanes, lane = slice(HALF, SIDE), lax.broadcasted_iota(jnp.int32, (1, TOK), 1)
    factor = jnp.where(lane < D_HEAD, SCALE, 1.0)
    for v in range(GROUP):
        k_t = col_block(data, other, v).T[:D_HEAD, :]
        p, ds = probs_of(s_tiles[1][v], dp_tiles[1][v], v, slice(0, SIDE))
        dkv_acc[:HALF] = both_grads(p, ds, v, slice(0, SIDE))
        dq = mm(k_t[:, :HALF], ds)
        p, ds = probs_of(s_tiles[2][v], dp_tiles[2][v], v, late_lanes)
        dkv_acc[HALF:] = both_grads(p, ds, v, late_lanes)
        dq = jnp.concatenate([dq[:, :HALF], dq[:, HALF:] + mm(k_t[:, HALF:], ds)], axis=1)
        dq_acc[v] = dq if v == 0 else dq_acc[v] + dq
        for u in range(v + 1, GROUP):
            p, ds = probs_of(s_tiles[0][below(v, u)], dp_tiles[0][below(v, u)], u, slice(0, SIDE))
            dq = mm(k_t, ds)
            dq_acc[u] = dq if v == 0 else dq_acc[u] + dq
            dkv_acc[...] += both_grads(p, ds, u, slice(0, SIDE))
        done = (dkv_acc[...] * factor).astype(BF).reshape(2, 2, QUAD, PART, 2 * D_HEAD)
        for half in range(2):
            chips = slice(v * PER + half * QUAD, v * PER + (half + 1) * QUAD)
            dkv_ref[chips] = done[half, 0]
            give_ref[chips, :PART, :] = done[half, 1]
    for u in range(GROUP):
        dq = (dq_acc[u] * SCALE).T.astype(BF).reshape(2, 2, QUAD, PART, D_HEAD)
        dq = jnp.concatenate([dq[..., : PART // 2, :], dq[..., PART // 2 :, :]], axis=4)
        for half in range(2):
            chips = slice(u * PER + half * QUAD, u * PER + (half + 1) * QUAD)
            dq_ref[chips] = dq[half, 0]
            give_ref[chips, PART:, :] = dq[half, 1]


def pair_body(at, dkv, dq, got, out_ref):
    core = at[2]
    half = PART // 2
    out_ref[:, :PART, :] = (dkv[...].astype(F32) + got[:, :PART, :].astype(F32)).astype(BF)
    out_ref[:, pl.ds(pl.multiple_of(PART + core * half, half), half), :] = dq[...]
    out_ref[:, pl.ds(pl.multiple_of(PART + (1 - core) * half, half), half), :] = got[:, PART:, :]


def sum_body(part, dq_ref, dk_ref, dv_ref):
    def cols_of(b, c):
        return sum(part[chip_of(b, r1, c), :PART, :].astype(F32) for r1 in range(2))

    def rows_of(b, r):
        lines = slice(PART + (r % 2) * (PART // 2), PART + (r % 2 + 1) * (PART // 2))
        both = sum(part[chip_of(b, r // 2, c), lines, :].astype(F32) for c in range(GROUP))
        return jnp.concatenate([both[:, :D_HEAD], both[:, D_HEAD:]], axis=0)

    for pair in range(2):
        lanes = slice(pair * 2 * D_HEAD, (pair + 1) * 2 * D_HEAD)
        heads = (2 * pair, 2 * pair + 1)
        for x in range(GROUP):
            toks = slice(x * PART, (x + 1) * PART)
            dkv = [cols_of(b, x) for b in heads]
            dq_ref[toks, lanes] = jnp.concatenate([rows_of(b, x) for b in heads], axis=1).astype(BF)
            dk_ref[toks, lanes] = jnp.concatenate([a[:, :D_HEAD] for a in dkv], axis=1).astype(BF)
            dv_ref[toks, lanes] = jnp.concatenate([a[:, D_HEAD:] for a in dkv], axis=1).astype(BF)


CHIP_AXES = ("b", "c1", "r1", "c0")


def swap(piece, axes):
    return lax.all_to_all(piece, axes, split_axis=0, concat_axis=0, tiled=True)


def meet(piece):
    return lax.ppermute(piece, "core", [(0, 1), (1, 0)])


def shards(queries, keys, values, out_grad):
    core = lax.axis_index("core")
    r = 2 * lax.axis_index("r1") + core
    c = 2 * lax.axis_index("c1") + lax.axis_index("c0")
    at = jnp.stack([r, c, core]).astype(jnp.int32)
    wide = GROUP * D_HEAD
    grad_parts = call(split_grad, shape(HEADS, TOK // HEADS, wide), [], out_grad)
    grad_local = swap(grad_parts, "head").reshape(TOK, wide)
    message = shape(CHIPS, 3 * PART, 2 * D_HEAD)
    stage = [pltpu.VMEM((GROUP, PART, 2 * D_HEAD), BF)]
    part = call(pack_body, message, stage, at, queries, keys, values)
    data = swap(call(add_grad, message, stage, at, grad_local, part), CHIP_AXES)
    other = meet(call(give_body, shape(CHIPS, 2 * PART, 2 * D_HEAD), [], data))
    stat = shape(GROUP, 2 * GROUP, SIDE, dtype=F32)
    tiles = [
        shape(FULL, SIDE, SIDE, dtype=F32),
        shape(GROUP, HALF, SIDE, dtype=F32),
        shape(GROUP, HALF, HALF, dtype=F32),
    ]
    stats, *saved = call(stats_body, [stat, *tiles, *tiles], [], at, data, other, micros=5)
    stats = swap(stats, ("c1", "c0"))
    half = PART // 2
    dkv, dq, give = call(
        grads_body,
        [
            shape(CHIPS, PART, 2 * D_HEAD),
            shape(CHIPS, half, 2 * D_HEAD),
            shape(CHIPS, PART + half, 2 * D_HEAD),
        ],
        [
            pltpu.VMEM(stat.shape[1:], F32),
            pltpu.VMEM((GROUP, SIDE, 2 * D_HEAD), BF),
            pltpu.VMEM((GROUP, SIDE, 2 * D_HEAD), BF),
            pltpu.VMEM((GROUP, D_HEAD, SIDE), F32),
            pltpu.VMEM((SIDE, 2 * D_HEAD), F32),
        ],
        data, other, stats, *saved,
        micros=7,
    )
    partial = call(
        pair_body, shape(CHIPS, 2 * PART, 2 * D_HEAD), [], at, dkv, dq, meet(give)
    )
    return tuple(call(sum_body, [shape(TOK, wide)] * 3, [], swap(partial, CHIP_AXES)))


def solution(mesh):
    ctx = (*CHIP_AXES, "core")
    split = Mesh(mesh.devices.reshape(4, 2, 2, 2, 2, HEADS), (*ctx, "head"))
    placed = (P(ctx, "head"), P(ctx, "head"), P(ctx, "head"), P((*ctx, "head"), None))
    return jax.shard_map(
        shards,
        mesh=split,
        in_specs=placed,
        out_specs=placed[:3],
        check_vma=False,
    )
```

```python
import functools

import jax
import jax.numpy as jnp
from jax import lax
from jax.experimental import pallas as pl
from jax.experimental.pallas import tpu as pltpu
from jax.sharding import Mesh
from jax.sharding import PartitionSpec as P

D_HEAD = 64
TOK = 128
GROUP = 4
SIDE = TOK * GROUP
SCALE = D_HEAD ** (-0.5)
EXP2_SCALE = SCALE * 1.4426950408889634
NEG = -1e30
FLOPS_PER_MICRO = 10**9
BF = jnp.bfloat16
F32 = jnp.float32

PART = TOK // GROUP
CHIPS = 32
HEADS = 8
PER = SIDE // PART // 2
HALF = SIDE // 2
QUAD = PER // 2
FULL = GROUP * (GROUP - 1) // 2


def chip_of(b, r1, c):
    return b * 8 + (c // 2) * 4 + r1 * 2 + c % 2


def call(body, out_shapes, scratch, *operands, micros=1, space=pltpu.VMEM, vmem=24):
    spaces = [pltpu.SMEM if x.dtype == jnp.int32 else space for x in operands]
    return pl.pallas_call(
        body,
        out_shape=out_shapes,
        in_specs=[pl.BlockSpec(memory_space=space) for space in spaces],
        out_specs=jax.tree.map(lambda _: pl.BlockSpec(memory_space=pltpu.VMEM), out_shapes),
        scratch_shapes=scratch,
        cost_estimate=pl.CostEstimate(
            flops=micros * FLOPS_PER_MICRO, bytes_accessed=2**20, transcendentals=0
        ),
        compiler_params=pltpu.CompilerParams(vmem_limit_bytes=vmem * 2**20),
    )(*operands)


def shape(*dims, dtype=BF):
    return jax.ShapeDtypeStruct(dims, dtype)


def split_grad(at, grad, keep_ref, give_ref):
    half = GROUP * GROUP * D_HEAD
    for out, side in ((keep_ref, at[3]), (give_ref, 1 - at[3])):
        out[...] = grad[:, pl.ds(pl.multiple_of(side * half, half), half)]


def regroup_grad(keep, got, out_ref):
    wide, few = GROUP * D_HEAD, TOK // HEADS
    for x in range(GROUP):
        out_ref[x, :few, :] = keep[:, x * wide : (x + 1) * wide]
        out_ref[x, few:, :] = got[:, x * wide : (x + 1) * wide]


def pack_body(q_hbm, k_hbm, v_hbm, out_ref, q_ref, k_ref, v_ref, sems):
    pairs = ((q_hbm, q_ref), (k_hbm, k_ref), (v_hbm, v_ref))
    copies = [pltpu.make_async_copy(*pair, sems.at[i]) for i, pair in enumerate(pairs)]
    for copy in copies:
        copy.start()
    for copy in copies:
        copy.wait()
    for b in range(GROUP):
        lanes = slice(b * D_HEAD, (b + 1) * D_HEAD)
        for i, halves_of in enumerate(((q_ref, q_ref), (k_ref, v_ref))):
            out_ref[i, b] = jnp.concatenate([ref[:, lanes] for ref in halves_of], axis=1)


def add_grad(at, g_ref, part_ref, out_ref, stage):
    core, few = at[2], TOK // HEADS
    first = lax.broadcasted_iota(jnp.int32, (few, 2 * D_HEAD), 1) < D_HEAD
    for b in range(GROUP):
        lanes = slice(b * D_HEAD, (b + 1) * D_HEAD)
        for x in range(GROUP):
            for side in range(2):
                block = g_ref[x, side * few : (side + 1) * few, lanes]
                block = jnp.concatenate([block, block], axis=1)
                r, line = 2 * (at[3] ^ side) + x // 2, (x % 2) * few
                tokens = pl.ds(pl.multiple_of(r * PART + line, few), few)
                stage[r, line : line + few, :] = jnp.where(first, part_ref[0, b, tokens, :], block)
        for r1 in range(2):
            keep, give = stage[2 * r1 + core], stage[2 * r1 + 1 - core]
            for c in range(GROUP):
                to = chip_of(b, r1, c)
                out_ref[to, :PART, :] = keep
                out_ref[to, PART : 2 * PART, :] = part_ref[1, b, c * PART : (c + 1) * PART, :]
                out_ref[to, 2 * PART :, :] = give


def give_body(data, give_ref):
    give_ref[...] = data[:, PART:, :]


def make_bias(at):
    r, c, core = at[0], at[1], at[2]

    def block_start(index):
        block = 2 * ((index // PART) % QUAD) + (core ^ index // (HALF // 2))
        return block * TOK + index % PART

    key_pos = block_start(lax.broadcasted_iota(jnp.int32, (HALF, 1), 0)) + c * PART
    query_pos = block_start(lax.broadcasted_iota(jnp.int32, (1, HALF), 1)) + r * PART
    return jnp.where(key_pos <= query_pos, 0.0, NEG)


def mm(a, b):
    return lax.dot_general(a, b, (((1,), (0,)), ((), ())), preferred_element_type=F32)


def blocks(own, other, at):
    return jnp.concatenate(
        [
            ref[at * PER + half * QUAD : at * PER + (half + 1) * QUAD, first : first + PART, :]
            .reshape(HALF // 2, 2 * D_HEAD)
            for half in range(2)
            for ref, first in (own, other)
        ],
        axis=0,
    )


def row_block(data, other, u):
    return blocks((data, 0), (other, PART), u)


def col_block(data, other, v):
    return blocks((data, PART), (other, 0), v)


def below(v, u):
    return u * (u - 1) // 2 + v


def halves(both, axis):
    first = lax.broadcasted_iota(jnp.int32, both.shape, axis) < D_HEAD
    zeros = jnp.zeros_like(both)
    return jnp.where(first, both, zeros), jnp.where(first, zeros, both)


def stats_body(at, data, other, out_ref, *saved):
    s_tiles, dp_tiles = saved[:3], saved[3:]
    bias = make_bias(at)

    def multiply(u):
        q_low, g_low = halves(row_block(data, other, u).T, 0)
        kv_low = col_block(data, other, u)
        s = mm(kv_low[:HALF], q_low) * EXP2_SCALE
        s = jnp.concatenate([s[:, :HALF] + bias, s[:, HALF:]], axis=1)
        s_tiles[1][u] = s
        dp_tiles[1][u] = mm(kv_low[:HALF], g_low)
        top = jnp.max(s, axis=0, keepdims=True)
        yield None
        late = mm(kv_low[HALF:], q_low[:, HALF:]) * EXP2_SCALE + bias
        s_tiles[2][u] = late
        dp_tiles[2][u] = mm(kv_low[HALF:], g_low[:, HALF:])
        late_top = jnp.max(late, axis=0, keepdims=True)
        top = jnp.concatenate([top[:, :HALF], jnp.maximum(top[:, HALF:], late_top)], axis=1)
        yield top
        for v in range(u):
            kv_low = col_block(data, other, v)
            s = mm(kv_low, q_low) * EXP2_SCALE
            s_tiles[0][below(v, u)] = s
            dp_tiles[0][below(v, u)] = mm(kv_low, g_low)
            top = jnp.maximum(top, jnp.max(s, axis=0, keepdims=True))
            yield top

    def add_up(u, top):
        def sums(s, dp, top):
            p = jnp.exp2(s - top)
            return jnp.sum(p, axis=0, keepdims=True), jnp.sum(p * dp, axis=0, keepdims=True)

        first = sums(s_tiles[1][u], dp_tiles[1][u], top)
        yield None
        late = sums(s_tiles[2][u], dp_tiles[2][u], top[:, HALF:])
        total, weighted = (
            jnp.concatenate([a[:, :HALF], a[:, HALF:] + b], axis=1) for a, b in zip(first, late)
        )
        for v in range(u):
            yield None
            more = sums(s_tiles[0][below(v, u)], dp_tiles[0][below(v, u)], top)
            total, weighted = total + more[0], weighted + more[1]
        for d in range(GROUP):
            out_ref[d, u : u + 1, :] = top + jnp.log2(total)
            out_ref[d, u + GROUP : u + GROUP + 1, :] = weighted / total

    behind = iter(())
    for u in reversed(range(GROUP)):
        for top in multiply(u):
            next(behind, None)
        for _ in behind:
            pass
        behind = add_up(u, top)
    for _ in behind:
        pass


def grads_body(data, other, stats, *rest):
    s_tiles, dp_tiles, (dkv_ref, dq_ref, give_ref) = rest[:3], rest[3:6], rest[6:9]
    row_ref, q_rows, g_rows, dq_acc, dkv_acc = rest[9:]
    logs = [stats[d, :GROUP, :] for d in range(GROUP)]
    top = functools.reduce(jnp.maximum, logs)
    weights = [jnp.exp2(one - top) for one in logs]
    total = sum(weights)
    row_ref[:GROUP, :] = top + jnp.log2(total)
    row_ref[GROUP:, :] = sum(w * stats[d, GROUP:, :] for d, w in enumerate(weights)) / total
    for u in range(GROUP):
        q_rows[u], g_rows[u] = halves(row_block(data, other, u), 1)

    def probs_of(s, dp, u, lanes):
        p = jnp.exp2(s - row_ref[u : u + 1, lanes])
        ds = p * (dp - row_ref[GROUP + u : GROUP + u + 1, lanes])
        return p.astype(BF), ds.astype(BF)

    def both_grads(p, ds, u, lanes):
        return mm(ds, q_rows[u, lanes, :]) + mm(p, g_rows[u, lanes, :])

    late_lanes, lane = slice(HALF, SIDE), lax.broadcasted_iota(jnp.int32, (1, TOK), 1)
    factor = jnp.where(lane < D_HEAD, SCALE, 1.0)
    for v in range(GROUP):
        k_t = col_block(data, other, v).T[:D_HEAD, :]
        p, ds = probs_of(s_tiles[1][v], dp_tiles[1][v], v, slice(0, SIDE))
        dkv_acc[:HALF] = both_grads(p, ds, v, slice(0, SIDE))
        dq = mm(k_t[:, :HALF], ds)
        p, ds = probs_of(s_tiles[2][v], dp_tiles[2][v], v, late_lanes)
        dkv_acc[HALF:] = both_grads(p, ds, v, late_lanes)
        dq = jnp.concatenate([dq[:, :HALF], dq[:, HALF:] + mm(k_t[:, HALF:], ds)], axis=1)
        dq_acc[v] = dq if v == 0 else dq_acc[v] + dq
        for u in range(v + 1, GROUP):
            p, ds = probs_of(s_tiles[0][below(v, u)], dp_tiles[0][below(v, u)], u, slice(0, SIDE))
            dq = mm(k_t, ds)
            dq_acc[u] = dq if v == 0 else dq_acc[u] + dq
            dkv_acc[...] += both_grads(p, ds, u, slice(0, SIDE))
        done = (dkv_acc[...] * factor).astype(BF).reshape(2, 2, QUAD, PART, 2 * D_HEAD)
        for half in range(2):
            chips = slice(v * PER + half * QUAD, v * PER + (half + 1) * QUAD)
            dkv_ref[chips] = done[half, 0]
            give_ref[chips, :PART, :] = done[half, 1]
    for u in range(GROUP):
        dq = (dq_acc[u] * SCALE).T.astype(BF).reshape(2, 2, QUAD, PART, D_HEAD)
        dq = jnp.concatenate([dq[..., : PART // 2, :], dq[..., PART // 2 :, :]], axis=4)
        for half in range(2):
            chips = slice(u * PER + half * QUAD, u * PER + (half + 1) * QUAD)
            dq_ref[chips] = dq[half, 0]
            give_ref[chips, PART:, :] = dq[half, 1]


def pair_body(at, dkv, dq, got, out_ref):
    core = at[2]
    half = PART // 2
    out_ref[:, :PART, :] = (dkv[...].astype(F32) + got[:, :PART, :].astype(F32)).astype(BF)
    out_ref[:, pl.ds(pl.multiple_of(PART + core * half, half), half), :] = dq[...]
    out_ref[:, pl.ds(pl.multiple_of(PART + (1 - core) * half, half), half), :] = got[:, PART:, :]


def sum_body(part, dq_ref, dk_ref, dv_ref):
    def cols_of(b, c):
        return sum(part[chip_of(b, r1, c), :PART, :].astype(F32) for r1 in range(2))

    def rows_of(b, r):
        lines = slice(PART + (r % 2) * (PART // 2), PART + (r % 2 + 1) * (PART // 2))
        both = sum(part[chip_of(b, r // 2, c), lines, :].astype(F32) for c in range(GROUP))
        return jnp.concatenate([both[:, :D_HEAD], both[:, D_HEAD:]], axis=0)

    for pair in range(2):
        lanes = slice(pair * 2 * D_HEAD, (pair + 1) * 2 * D_HEAD)
        heads = (2 * pair, 2 * pair + 1)
        for x in range(GROUP):
            toks = slice(x * PART, (x + 1) * PART)
            dkv = [cols_of(b, x) for b in heads]
            dq_ref[toks, lanes] = jnp.concatenate([rows_of(b, x) for b in heads], axis=1).astype(BF)
            dk_ref[toks, lanes] = jnp.concatenate([a[:, :D_HEAD] for a in dkv], axis=1).astype(BF)
            dv_ref[toks, lanes] = jnp.concatenate([a[:, D_HEAD:] for a in dkv], axis=1).astype(BF)


CHIP_AXES = ("b", "c1", "r1", "c0")


def swap(piece, axes):
    return lax.all_to_all(piece, axes, split_axis=0, concat_axis=0, tiled=True)


def meet(piece, axis):
    return lax.ppermute(piece, axis, [(0, 1), (1, 0)])


def shards(queries, keys, values, out_grad):
    core = lax.axis_index("core")
    r = 2 * lax.axis_index("r1") + core
    c = 2 * lax.axis_index("c1") + lax.axis_index("c0")
    at = jnp.stack([r, c, core, lax.axis_index("zhi")]).astype(jnp.int32)
    wide = GROUP * D_HEAD
    few = TOK // HEADS
    keep, give = call(split_grad, [shape(few, GROUP * wide)] * 2, [], at, out_grad)
    regrouped = call(regroup_grad, shape(GROUP, 2 * few, wide), [], keep, meet(give, "zhi"))
    grad_local = swap(regrouped, "x")
    message = shape(CHIPS, 3 * PART, 2 * D_HEAD)
    local = [pltpu.VMEM((TOK, wide), BF)] * 3
    part = call(
        pack_body,
        shape(2, GROUP, TOK, 2 * D_HEAD),
        [*local, pltpu.SemaphoreType.DMA((3,))],
        queries, keys, values,
        space=pl.ANY,
        vmem=60,
    )
    stage = pltpu.VMEM((GROUP, PART, 2 * D_HEAD), BF)
    data = swap(call(add_grad, message, [stage], at, grad_local, part), CHIP_AXES)
    other = meet(call(give_body, shape(CHIPS, 2 * PART, 2 * D_HEAD), [], data), "core")
    stat = shape(GROUP, 2 * GROUP, SIDE, dtype=F32)
    tiles = [
        shape(FULL, SIDE, SIDE, dtype=F32),
        shape(GROUP, HALF, SIDE, dtype=F32),
        shape(GROUP, HALF, HALF, dtype=F32),
    ]
    stats, *saved = call(stats_body, [stat, *tiles, *tiles], [], at, data, other, micros=5)
    stats = swap(stats, ("c1", "c0"))
    half = PART // 2
    dkv, dq, give = call(
        grads_body,
        [
            shape(CHIPS, PART, 2 * D_HEAD),
            shape(CHIPS, half, 2 * D_HEAD),
            shape(CHIPS, PART + half, 2 * D_HEAD),
        ],
        [
            pltpu.VMEM(stat.shape[1:], F32),
            pltpu.VMEM((GROUP, SIDE, 2 * D_HEAD), BF),
            pltpu.VMEM((GROUP, SIDE, 2 * D_HEAD), BF),
            pltpu.VMEM((GROUP, D_HEAD, SIDE), F32),
            pltpu.VMEM((SIDE, 2 * D_HEAD), F32),
        ],
        data, other, stats, *saved,
        micros=7,
    )
    partial = call(
        pair_body, shape(CHIPS, 2 * PART, 2 * D_HEAD), [], at, dkv, dq, meet(give, "core")
    )
    return tuple(call(sum_body, [shape(TOK, wide)] * 3, [], swap(partial, CHIP_AXES)))


def solution(mesh):
    ctx = (*CHIP_AXES, "core")
    heads = ("zhi", "x")
    split = Mesh(mesh.devices.reshape(4, 2, 2, 2, 2, 2, 4), (*ctx, *heads))
    placed = (P(ctx, heads), P(ctx, heads), P(ctx, heads), P((*ctx, *heads), None))
    return jax.shard_map(
        shards,
        mesh=split,
        in_specs=placed,
        out_specs=placed[:3],
        check_vma=False,
    )
```

```python
import functools

import jax
import jax.numpy as jnp
from jax import lax
from jax.experimental import pallas as pl
from jax.experimental.pallas import tpu as pltpu
from jax.sharding import Mesh
from jax.sharding import PartitionSpec as P

D_HEAD = 64
TOK = 128
GROUP = 4
SIDE = TOK * GROUP
SCALE = D_HEAD ** (-0.5)
EXP2_SCALE = SCALE * 1.4426950408889634
NEG = -1e30
FLOPS_PER_MICRO = 10**9
BF = jnp.bfloat16
F32 = jnp.float32

PART = TOK // GROUP
CHIPS = 32
HEADS = 8
PER = SIDE // PART // 2
HALF = SIDE // 2
QUAD = PER // 2
FULL = GROUP * (GROUP - 1) // 2


def chip_of(b, r1, c):
    return (r1 * 2 + c % 2) * 8 + b * 2 + c // 2


def line_of(u, half):
    return [z * 8 + 2 * u + half for z in range(QUAD)]


def call(body, out_shapes, scratch, *operands, micros=1, space=pltpu.VMEM, vmem=24):
    spaces = [pltpu.SMEM if x.dtype == jnp.int32 else space for x in operands]
    return pl.pallas_call(
        body,
        out_shape=out_shapes,
        in_specs=[pl.BlockSpec(memory_space=space) for space in spaces],
        out_specs=jax.tree.map(lambda _: pl.BlockSpec(memory_space=pltpu.VMEM), out_shapes),
        scratch_shapes=scratch,
        cost_estimate=pl.CostEstimate(
            flops=micros * FLOPS_PER_MICRO, bytes_accessed=2**20, transcendentals=0
        ),
        compiler_params=pltpu.CompilerParams(vmem_limit_bytes=vmem * 2**20),
    )(*operands)


def shape(*dims, dtype=BF):
    return jax.ShapeDtypeStruct(dims, dtype)


def split_grad(grad, out_ref):
    for g in range(HEADS):
        out_ref[g] = grad[:, g * GROUP * D_HEAD : (g + 1) * GROUP * D_HEAD]


def pack_body(at, q_ref, k_ref, v_ref, out_ref, stage):
    core = at[2]
    for b in range(GROUP):
        lanes = slice(b * D_HEAD, (b + 1) * D_HEAD)
        both = jnp.concatenate([k_ref[:, lanes], v_ref[:, lanes]], axis=1)
        rows = jnp.concatenate([q_ref[:, lanes], q_ref[:, lanes]], axis=1)
        stage[...] = rows.reshape(GROUP, PART, 2 * D_HEAD)
        for r1 in range(2):
            keep, give = stage[2 * r1 + core], stage[2 * r1 + 1 - core]
            for c in range(GROUP):
                to = chip_of(b, r1, c)
                out_ref[to, :PART, :] = keep
                out_ref[to, PART : 2 * PART, :] = both[c * PART : (c + 1) * PART, :]
                out_ref[to, 2 * PART :, :] = give


def add_grad(at, g_ref, part_ref, out_ref, stage):
    core = at[2]
    first = lax.broadcasted_iota(jnp.int32, (PART, 2 * D_HEAD), 1) < D_HEAD
    for b in range(GROUP):
        lanes = slice(b * D_HEAD, (b + 1) * D_HEAD)
        rows = jnp.concatenate([g_ref[:, lanes], g_ref[:, lanes]], axis=1)
        stage[...] = rows.reshape(GROUP, PART, 2 * D_HEAD)
        for r1 in range(2):
            keep, give = stage[2 * r1 + core], stage[2 * r1 + 1 - core]
            for c in range(GROUP):
                to = chip_of(b, r1, c)
                out_ref[to, :PART, :] = jnp.where(first, part_ref[to, :PART, :], keep)
                out_ref[to, PART : 2 * PART, :] = part_ref[to, PART : 2 * PART, :]
                out_ref[to, 2 * PART :, :] = jnp.where(first, part_ref[to, 2 * PART :, :], give)


def give_body(data, give_ref):
    give_ref[...] = data[:, PART:, :]


def make_bias(at):
    r, c, core = at[0], at[1], at[2]

    def block_start(index):
        block = 2 * ((index // PART) % QUAD) + (core ^ index // (HALF // 2))
        return block * TOK + index % PART

    key_pos = block_start(lax.broadcasted_iota(jnp.int32, (HALF, 1), 0)) + c * PART
    query_pos = block_start(lax.broadcasted_iota(jnp.int32, (1, HALF), 1)) + r * PART
    return jnp.where(key_pos <= query_pos, 0.0, NEG)


def mm(a, b):
    return lax.dot_general(a, b, (((1,), (0,)), ((), ())), preferred_element_type=F32)


def blocks(own, other, at):
    return jnp.concatenate(
        [
            ref[chip, first : first + PART, :]
            for half in range(2)
            for ref, first in (own, other)
            for chip in line_of(at, half)
        ],
        axis=0,
    )


def row_block(data, other, u):
    return blocks((data, 0), (other, PART), u)


def col_block(data, other, v):
    return blocks((data, PART), (other, 0), v)


def below(v, u):
    return u * (u - 1) // 2 + v


def halves(both, axis):
    first = lax.broadcasted_iota(jnp.int32, both.shape, axis) < D_HEAD
    zeros = jnp.zeros_like(both)
    return jnp.where(first, both, zeros), jnp.where(first, zeros, both)


def stats_body(at, data, other, out_ref, *saved):
    s_tiles, dp_tiles = saved[:3], saved[3:]
    bias = make_bias(at)

    def multiply(u):
        q_low, g_low = halves(row_block(data, other, u).T, 0)
        kv_low = col_block(data, other, u)
        s = mm(kv_low[:HALF], q_low) * EXP2_SCALE
        s = jnp.concatenate([s[:, :HALF] + bias, s[:, HALF:]], axis=1)
        s_tiles[1][u] = s
        dp_tiles[1][u] = mm(kv_low[:HALF], g_low)
        top = jnp.max(s, axis=0, keepdims=True)
        yield None
        late = mm(kv_low[HALF:], q_low[:, HALF:]) * EXP2_SCALE + bias
        s_tiles[2][u] = late
        dp_tiles[2][u] = mm(kv_low[HALF:], g_low[:, HALF:])
        late_top = jnp.max(late, axis=0, keepdims=True)
        top = jnp.concatenate([top[:, :HALF], jnp.maximum(top[:, HALF:], late_top)], axis=1)
        yield top
        for v in range(u):
            kv_low = col_block(data, other, v)
            s = mm(kv_low, q_low) * EXP2_SCALE
            s_tiles[0][below(v, u)] = s
            dp_tiles[0][below(v, u)] = mm(kv_low, g_low)
            top = jnp.maximum(top, jnp.max(s, axis=0, keepdims=True))
            yield top

    def add_up(u, top):
        def sums(s, dp, top):
            p = jnp.exp2(s - top)
            return jnp.sum(p, axis=0, keepdims=True), jnp.sum(p * dp, axis=0, keepdims=True)

        first = sums(s_tiles[1][u], dp_tiles[1][u], top)
        yield None
        late = sums(s_tiles[2][u], dp_tiles[2][u], top[:, HALF:])
        total, weighted = (
            jnp.concatenate([a[:, :HALF], a[:, HALF:] + b], axis=1) for a, b in zip(first, late)
        )
        for v in range(u):
            yield None
            more = sums(s_tiles[0][below(v, u)], dp_tiles[0][below(v, u)], top)
            total, weighted = total + more[0], weighted + more[1]
        for d in range(GROUP):
            out_ref[d, u : u + 1, :] = top + jnp.log2(total)
            out_ref[d, u + GROUP : u + GROUP + 1, :] = weighted / total

    behind = iter(())
    for u in reversed(range(GROUP)):
        for top in multiply(u):
            next(behind, None)
        for _ in behind:
            pass
        behind = add_up(u, top)
    for _ in behind:
        pass


def grads_body(data, other, stats, *rest):
    s_tiles, dp_tiles, (dkv_ref, dq_ref, give_ref) = rest[:3], rest[3:6], rest[6:9]
    row_ref, q_rows, g_rows, dq_acc, dkv_acc = rest[9:]
    logs = [stats[d, :GROUP, :] for d in range(GROUP)]
    top = functools.reduce(jnp.maximum, logs)
    weights = [jnp.exp2(one - top) for one in logs]
    total = sum(weights)
    row_ref[:GROUP, :] = top + jnp.log2(total)
    row_ref[GROUP:, :] = sum(w * stats[d, GROUP:, :] for d, w in enumerate(weights)) / total
    for u in range(GROUP):
        q_rows[u], g_rows[u] = halves(row_block(data, other, u), 1)

    def probs_of(s, dp, u, lanes):
        p = jnp.exp2(s - row_ref[u : u + 1, lanes])
        ds = p * (dp - row_ref[GROUP + u : GROUP + u + 1, lanes])
        return p.astype(BF), ds.astype(BF)

    def both_grads(p, ds, u, lanes):
        return mm(ds, q_rows[u, lanes, :]) + mm(p, g_rows[u, lanes, :])

    late_lanes, lane = slice(HALF, SIDE), lax.broadcasted_iota(jnp.int32, (1, TOK), 1)
    factor = jnp.where(lane < D_HEAD, SCALE, 1.0)
    for v in range(GROUP):
        k_t = col_block(data, other, v).T[:D_HEAD, :]
        p, ds = probs_of(s_tiles[1][v], dp_tiles[1][v], v, slice(0, SIDE))
        dkv_acc[:HALF] = both_grads(p, ds, v, slice(0, SIDE))
        dq = mm(k_t[:, :HALF], ds)
        p, ds = probs_of(s_tiles[2][v], dp_tiles[2][v], v, late_lanes)
        dkv_acc[HALF:] = both_grads(p, ds, v, late_lanes)
        dq = jnp.concatenate([dq[:, :HALF], dq[:, HALF:] + mm(k_t[:, HALF:], ds)], axis=1)
        dq_acc[v] = dq if v == 0 else dq_acc[v] + dq
        for u in range(v + 1, GROUP):
            p, ds = probs_of(s_tiles[0][below(v, u)], dp_tiles[0][below(v, u)], u, slice(0, SIDE))
            dq = mm(k_t, ds)
            dq_acc[u] = dq if v == 0 else dq_acc[u] + dq
            dkv_acc[...] += both_grads(p, ds, u, slice(0, SIDE))
        done = (dkv_acc[...] * factor).astype(BF).reshape(2, 2, QUAD, PART, 2 * D_HEAD)
        for half in range(2):
            for i, chip in enumerate(line_of(v, half)):
                dkv_ref[chip] = done[half, 0, i]
                give_ref[chip, :PART, :] = done[half, 1, i]
    for u in range(GROUP):
        dq = (dq_acc[u] * SCALE).T.astype(BF).reshape(2, 2, QUAD, PART, D_HEAD)
        dq = jnp.concatenate([dq[..., : PART // 2, :], dq[..., PART // 2 :, :]], axis=4)
        for half in range(2):
            for i, chip in enumerate(line_of(u, half)):
                dq_ref[chip] = dq[half, 0, i]
                give_ref[chip, PART:, :] = dq[half, 1, i]


def pair_body(at, dkv, dq, got, out_ref):
    core = at[2]
    half = PART // 2
    out_ref[:, :PART, :] = (dkv[...].astype(F32) + got[:, :PART, :].astype(F32)).astype(BF)
    out_ref[:, pl.ds(pl.multiple_of(PART + core * half, half), half), :] = dq[...]
    out_ref[:, pl.ds(pl.multiple_of(PART + (1 - core) * half, half), half), :] = got[:, PART:, :]


def sum_body(part, dq_ref, dk_ref, dv_ref):
    def cols_of(b, c):
        return sum(part[chip_of(b, r1, c), :PART, :].astype(F32) for r1 in range(2))

    def rows_of(b, r):
        lines = slice(PART + (r % 2) * (PART // 2), PART + (r % 2 + 1) * (PART // 2))
        both = sum(part[chip_of(b, r // 2, c), lines, :].astype(F32) for c in range(GROUP))
        return jnp.concatenate([both[:, :D_HEAD], both[:, D_HEAD:]], axis=0)

    for pair in range(2):
        lanes = slice(pair * 2 * D_HEAD, (pair + 1) * 2 * D_HEAD)
        heads = (2 * pair, 2 * pair + 1)
        for x in range(GROUP):
            toks = slice(x * PART, (x + 1) * PART)
            dkv = [cols_of(b, x) for b in heads]
            dq_ref[toks, lanes] = jnp.concatenate([rows_of(b, x) for b in heads], axis=1).astype(BF)
            dk_ref[toks, lanes] = jnp.concatenate([a[:, :D_HEAD] for a in dkv], axis=1).astype(BF)
            dv_ref[toks, lanes] = jnp.concatenate([a[:, D_HEAD:] for a in dkv], axis=1).astype(BF)


CHIP_AXES = ("b", "c1", "r1", "c0")
SWAP_AXES = ("r1", "c0", "b", "c1")


def swap(piece, axes):
    return lax.all_to_all(piece, axes, split_axis=0, concat_axis=0, tiled=True)


def meet(piece):
    return lax.ppermute(piece, "core", [(0, 1), (1, 0)])


def shards(queries, keys, values, out_grad):
    core = lax.axis_index("core")
    r = 2 * lax.axis_index("r1") + core
    c = 2 * lax.axis_index("c1") + lax.axis_index("c0")
    at = jnp.stack([r, c, core]).astype(jnp.int32)
    wide = GROUP * D_HEAD
    grad_parts = call(split_grad, shape(HEADS, TOK // HEADS, wide), [], out_grad)
    grad_local = swap(grad_parts, "head").reshape(TOK, wide)
    message = shape(CHIPS, 3 * PART, 2 * D_HEAD)
    stage = [pltpu.VMEM((GROUP, PART, 2 * D_HEAD), BF)]
    part = call(pack_body, message, stage, at, queries, keys, values)
    data = swap(call(add_grad, message, stage, at, grad_local, part), SWAP_AXES)
    other = meet(call(give_body, shape(CHIPS, 2 * PART, 2 * D_HEAD), [], data))
    stat = shape(GROUP, 2 * GROUP, SIDE, dtype=F32)
    tiles = [
        shape(FULL, SIDE, SIDE, dtype=F32),
        shape(GROUP, HALF, SIDE, dtype=F32),
        shape(GROUP, HALF, HALF, dtype=F32),
    ]
    stats, *saved = call(stats_body, [stat, *tiles, *tiles], [], at, data, other, micros=5)
    stats = swap(stats, ("c1", "c0"))
    half = PART // 2
    dkv, dq, give = call(
        grads_body,
        [
            shape(CHIPS, PART, 2 * D_HEAD),
            shape(CHIPS, half, 2 * D_HEAD),
            shape(CHIPS, PART + half, 2 * D_HEAD),
        ],
        [
            pltpu.VMEM(stat.shape[1:], F32),
            pltpu.VMEM((GROUP, SIDE, 2 * D_HEAD), BF),
            pltpu.VMEM((GROUP, SIDE, 2 * D_HEAD), BF),
            pltpu.VMEM((GROUP, D_HEAD, SIDE), F32),
            pltpu.VMEM((SIDE, 2 * D_HEAD), F32),
        ],
        data, other, stats, *saved,
        micros=7,
    )
    partial = call(
        pair_body, shape(CHIPS, 2 * PART, 2 * D_HEAD), [], at, dkv, dq, meet(give)
    )
    return tuple(call(sum_body, [shape(TOK, wide)] * 3, [], swap(partial, SWAP_AXES)))


def solution(mesh):
    ctx = (*CHIP_AXES, "core")
    split = Mesh(mesh.devices.reshape(4, 2, 2, 2, 2, HEADS), (*ctx, "head"))
    placed = (P(ctx, "head"), P(ctx, "head"), P(ctx, "head"), P((*ctx, "head"), None))
    return jax.shard_map(
        shards,
        mesh=split,
        in_specs=placed,
        out_specs=placed[:3],
        check_vma=False,
    )
```

```python
import functools

import jax
import jax.numpy as jnp
from jax import lax
from jax.experimental import pallas as pl
from jax.experimental.pallas import tpu as pltpu
from jax.sharding import Mesh
from jax.sharding import PartitionSpec as P

D_HEAD = 64
TOK = 128
GROUP = 4
SIDE = TOK * GROUP
SCALE = D_HEAD ** (-0.5)
EXP2_SCALE = SCALE * 1.4426950408889634
NEG = -1e30
FLOPS_PER_MICRO = 10**9
BF = jnp.bfloat16
F32 = jnp.float32

PART = TOK // GROUP
CHIPS = 32
HEADS = 8
PER = SIDE // PART // 2
HALF = SIDE // 2
QUAD = PER // 2
FULL = GROUP * (GROUP - 1) // 2


def chip_of(b, r1, c):
    return b * 8 + (c // 2) * 4 + r1 * 2 + c % 2


def call(body, out_shapes, scratch, *operands, micros=1, space=pltpu.VMEM, vmem=24):
    spaces = [pltpu.SMEM if x.dtype == jnp.int32 else space for x in operands]
    return pl.pallas_call(
        body,
        out_shape=out_shapes,
        in_specs=[pl.BlockSpec(memory_space=space) for space in spaces],
        out_specs=jax.tree.map(lambda _: pl.BlockSpec(memory_space=pltpu.VMEM), out_shapes),
        scratch_shapes=scratch,
        cost_estimate=pl.CostEstimate(
            flops=micros * FLOPS_PER_MICRO, bytes_accessed=2**20, transcendentals=0
        ),
        compiler_params=pltpu.CompilerParams(vmem_limit_bytes=vmem * 2**20),
    )(*operands)


def shape(*dims, dtype=BF):
    return jax.ShapeDtypeStruct(dims, dtype)


def split_grad(grad, out_ref, sems):
    wide = GROUP * D_HEAD
    copies = [
        pltpu.make_async_copy(grad.at[:, pl.ds(g * wide, wide)], out_ref.at[g], sems.at[g])
        for g in range(HEADS)
    ]
    for copy in copies:
        copy.start()
    for copy in copies:
        copy.wait()


def pack_body(at, q_ref, k_ref, v_ref, out_ref, stage):
    core = at[2]
    for b in range(GROUP):
        lanes = slice(b * D_HEAD, (b + 1) * D_HEAD)
        both = jnp.concatenate([k_ref[:, lanes], v_ref[:, lanes]], axis=1)
        rows = jnp.concatenate([q_ref[:, lanes], q_ref[:, lanes]], axis=1)
        stage[...] = rows.reshape(GROUP, PART, 2 * D_HEAD)
        for r1 in range(2):
            keep, give = stage[2 * r1 + core], stage[2 * r1 + 1 - core]
            for c in range(GROUP):
                to = chip_of(b, r1, c)
                out_ref[to, :PART, :] = keep
                out_ref[to, PART : 2 * PART, :] = both[c * PART : (c + 1) * PART, :]
                out_ref[to, 2 * PART :, :] = give


def add_grad(at, g_ref, part_ref, out_ref, stage):
    core = at[2]
    first = lax.broadcasted_iota(jnp.int32, (PART, 2 * D_HEAD), 1) < D_HEAD
    for b in range(GROUP):
        lanes = slice(b * D_HEAD, (b + 1) * D_HEAD)
        rows = jnp.concatenate([g_ref[:, lanes], g_ref[:, lanes]], axis=1)
        stage[...] = rows.reshape(GROUP, PART, 2 * D_HEAD)
        for r1 in range(2):
            keep, give = stage[2 * r1 + core], stage[2 * r1 + 1 - core]
            for c in range(GROUP):
                to = chip_of(b, r1, c)
                out_ref[to, :PART, :] = jnp.where(first, part_ref[to, :PART, :], keep)
                out_ref[to, PART : 2 * PART, :] = part_ref[to, PART : 2 * PART, :]
                out_ref[to, 2 * PART :, :] = jnp.where(first, part_ref[to, 2 * PART :, :], give)


def give_body(data, give_ref):
    give_ref[...] = data[:, PART:, :]


def make_bias(at):
    r, c, core = at[0], at[1], at[2]

    def block_start(index):
        block = 2 * ((index // PART) % QUAD) + (core ^ index // (HALF // 2))
        return block * TOK + index % PART

    key_pos = block_start(lax.broadcasted_iota(jnp.int32, (HALF, 1), 0)) + c * PART
    query_pos = block_start(lax.broadcasted_iota(jnp.int32, (1, HALF), 1)) + r * PART
    return jnp.where(key_pos <= query_pos, 0.0, NEG)


def mm(a, b):
    return lax.dot_general(a, b, (((1,), (0,)), ((), ())), preferred_element_type=F32)


def blocks(own, other, at):
    return jnp.concatenate(
        [
            ref[at * PER + half * QUAD : at * PER + (half + 1) * QUAD, first : first + PART, :]
            .reshape(HALF // 2, 2 * D_HEAD)
            for half in range(2)
            for ref, first in (own, other)
        ],
        axis=0,
    )


def row_block(data, other, u):
    return blocks((data, 0), (other, PART), u)


def col_block(data, other, v):
    return blocks((data, PART), (other, 0), v)


def below(v, u):
    return u * (u - 1) // 2 + v


def halves(both, axis):
    first = lax.broadcasted_iota(jnp.int32, both.shape, axis) < D_HEAD
    zeros = jnp.zeros_like(both)
    return jnp.where(first, both, zeros), jnp.where(first, zeros, both)


def stats_body(at, data, other, out_ref, *saved):
    s_tiles, dp_tiles = saved[:3], saved[3:]
    bias = make_bias(at)

    def multiply(u):
        q_low, g_low = halves(row_block(data, other, u).T, 0)
        kv_low = col_block(data, other, u)
        s = mm(kv_low[:HALF], q_low) * EXP2_SCALE
        s = jnp.concatenate([s[:, :HALF] + bias, s[:, HALF:]], axis=1)
        s_tiles[1][u] = s
        dp_tiles[1][u] = mm(kv_low[:HALF], g_low)
        top = jnp.max(s, axis=0, keepdims=True)
        yield None
        late = mm(kv_low[HALF:], q_low[:, HALF:]) * EXP2_SCALE + bias
        s_tiles[2][u] = late
        dp_tiles[2][u] = mm(kv_low[HALF:], g_low[:, HALF:])
        late_top = jnp.max(late, axis=0, keepdims=True)
        top = jnp.concatenate([top[:, :HALF], jnp.maximum(top[:, HALF:], late_top)], axis=1)
        yield top
        for v in range(u):
            kv_low = col_block(data, other, v)
            s = mm(kv_low, q_low) * EXP2_SCALE
            s_tiles[0][below(v, u)] = s
            dp_tiles[0][below(v, u)] = mm(kv_low, g_low)
            top = jnp.maximum(top, jnp.max(s, axis=0, keepdims=True))
            yield top

    def add_up(u, top):
        def sums(s, dp, top):
            p = jnp.exp2(s - top)
            return jnp.sum(p, axis=0, keepdims=True), jnp.sum(p * dp, axis=0, keepdims=True)

        first = sums(s_tiles[1][u], dp_tiles[1][u], top)
        yield None
        late = sums(s_tiles[2][u], dp_tiles[2][u], top[:, HALF:])
        total, weighted = (
            jnp.concatenate([a[:, :HALF], a[:, HALF:] + b], axis=1) for a, b in zip(first, late)
        )
        for v in range(u):
            yield None
            more = sums(s_tiles[0][below(v, u)], dp_tiles[0][below(v, u)], top)
            total, weighted = total + more[0], weighted + more[1]
        for d in range(GROUP):
            out_ref[d, u : u + 1, :] = top + jnp.log2(total)
            out_ref[d, u + GROUP : u + GROUP + 1, :] = weighted / total

    behind = iter(())
    for u in reversed(range(GROUP)):
        for top in multiply(u):
            next(behind, None)
        for _ in behind:
            pass
        behind = add_up(u, top)
    for _ in behind:
        pass


def grads_body(data, other, stats, *rest):
    s_tiles, dp_tiles, (dkv_ref, dq_ref, give_ref) = rest[:3], rest[3:6], rest[6:9]
    row_ref, q_rows, g_rows, dq_acc, dkv_acc = rest[9:]
    logs = [stats[d, :GROUP, :] for d in range(GROUP)]
    top = functools.reduce(jnp.maximum, logs)
    weights = [jnp.exp2(one - top) for one in logs]
    total = sum(weights)
    row_ref[:GROUP, :] = top + jnp.log2(total)
    row_ref[GROUP:, :] = sum(w * stats[d, GROUP:, :] for d, w in enumerate(weights)) / total
    for u in range(GROUP):
        q_rows[u], g_rows[u] = halves(row_block(data, other, u), 1)

    def probs_of(s, dp, u, lanes):
        p = jnp.exp2(s - row_ref[u : u + 1, lanes])
        ds = p * (dp - row_ref[GROUP + u : GROUP + u + 1, lanes])
        return p.astype(BF), ds.astype(BF)

    def both_grads(p, ds, u, lanes):
        return mm(ds, q_rows[u, lanes, :]) + mm(p, g_rows[u, lanes, :])

    late_lanes, lane = slice(HALF, SIDE), lax.broadcasted_iota(jnp.int32, (1, TOK), 1)
    factor = jnp.where(lane < D_HEAD, SCALE, 1.0)
    for v in range(GROUP):
        k_t = col_block(data, other, v).T[:D_HEAD, :]
        p, ds = probs_of(s_tiles[1][v], dp_tiles[1][v], v, slice(0, SIDE))
        dkv_acc[:HALF] = both_grads(p, ds, v, slice(0, SIDE))
        dq = mm(k_t[:, :HALF], ds)
        p, ds = probs_of(s_tiles[2][v], dp_tiles[2][v], v, late_lanes)
        dkv_acc[HALF:] = both_grads(p, ds, v, late_lanes)
        dq = jnp.concatenate([dq[:, :HALF], dq[:, HALF:] + mm(k_t[:, HALF:], ds)], axis=1)
        dq_acc[v] = dq if v == 0 else dq_acc[v] + dq
        for u in range(v + 1, GROUP):
            p, ds = probs_of(s_tiles[0][below(v, u)], dp_tiles[0][below(v, u)], u, slice(0, SIDE))
            dq = mm(k_t, ds)
            dq_acc[u] = dq if v == 0 else dq_acc[u] + dq
            dkv_acc[...] += both_grads(p, ds, u, slice(0, SIDE))
        done = (dkv_acc[...] * factor).astype(BF).reshape(2, 2, QUAD, PART, 2 * D_HEAD)
        for half in range(2):
            chips = slice(v * PER + half * QUAD, v * PER + (half + 1) * QUAD)
            dkv_ref[chips] = done[half, 0]
            give_ref[chips, :PART, :] = done[half, 1]
    for u in range(GROUP):
        dq = (dq_acc[u] * SCALE).T.astype(BF).reshape(2, 2, QUAD, PART, D_HEAD)
        dq = jnp.concatenate([dq[..., : PART // 2, :], dq[..., PART // 2 :, :]], axis=4)
        for half in range(2):
            chips = slice(u * PER + half * QUAD, u * PER + (half + 1) * QUAD)
            dq_ref[chips] = dq[half, 0]
            give_ref[chips, PART:, :] = dq[half, 1]


def pair_body(at, dkv, dq, got, out_ref):
    core = at[2]
    half = PART // 2
    out_ref[:, :PART, :] = (dkv[...].astype(F32) + got[:, :PART, :].astype(F32)).astype(BF)
    out_ref[:, pl.ds(pl.multiple_of(PART + core * half, half), half), :] = dq[...]
    out_ref[:, pl.ds(pl.multiple_of(PART + (1 - core) * half, half), half), :] = got[:, PART:, :]


def sum_body(part, dq_ref, dk_ref, dv_ref):
    def cols_of(b, c):
        return sum(part[chip_of(b, r1, c), :PART, :].astype(F32) for r1 in range(2))

    def rows_of(b, r):
        lines = slice(PART + (r % 2) * (PART // 2), PART + (r % 2 + 1) * (PART // 2))
        both = sum(part[chip_of(b, r // 2, c), lines, :].astype(F32) for c in range(GROUP))
        return jnp.concatenate([both[:, :D_HEAD], both[:, D_HEAD:]], axis=0)

    for pair in range(2):
        lanes = slice(pair * 2 * D_HEAD, (pair + 1) * 2 * D_HEAD)
        heads = (2 * pair, 2 * pair + 1)
        for x in range(GROUP):
            toks = slice(x * PART, (x + 1) * PART)
            dkv = [cols_of(b, x) for b in heads]
            dq_ref[toks, lanes] = jnp.concatenate([rows_of(b, x) for b in heads], axis=1).astype(BF)
            dk_ref[toks, lanes] = jnp.concatenate([a[:, :D_HEAD] for a in dkv], axis=1).astype(BF)
            dv_ref[toks, lanes] = jnp.concatenate([a[:, D_HEAD:] for a in dkv], axis=1).astype(BF)


CHIP_AXES = ("b", "c1", "r1", "c0")


def swap(piece, axes):
    return lax.all_to_all(piece, axes, split_axis=0, concat_axis=0, tiled=True)


def meet(piece):
    return lax.ppermute(piece, "core", [(0, 1), (1, 0)])


def shards(queries, keys, values, out_grad):
    core = lax.axis_index("core")
    r = 2 * lax.axis_index("r1") + core
    c = 2 * lax.axis_index("c1") + lax.axis_index("c0")
    at = jnp.stack([r, c, core]).astype(jnp.int32)
    wide = GROUP * D_HEAD
    grad_parts = pl.pallas_call(
        split_grad,
        out_shape=shape(HEADS, TOK // HEADS, wide),
        in_specs=[pl.BlockSpec(memory_space=pl.ANY)],
        out_specs=pl.BlockSpec(memory_space=pl.ANY),
        scratch_shapes=[pltpu.SemaphoreType.DMA((HEADS,))],
        compiler_params=pltpu.CompilerParams(vmem_limit_bytes=60 * 2**20),
    )(out_grad)
    grad_local = swap(grad_parts, "head").reshape(TOK, wide)
    message = shape(CHIPS, 3 * PART, 2 * D_HEAD)
    stage = [pltpu.VMEM((GROUP, PART, 2 * D_HEAD), BF)]
    part = call(pack_body, message, stage, at, queries, keys, values)
    data = swap(call(add_grad, message, stage, at, grad_local, part), CHIP_AXES)
    other = meet(call(give_body, shape(CHIPS, 2 * PART, 2 * D_HEAD), [], data))
    stat = shape(GROUP, 2 * GROUP, SIDE, dtype=F32)
    tiles = [
        shape(FULL, SIDE, SIDE, dtype=F32),
        shape(GROUP, HALF, SIDE, dtype=F32),
        shape(GROUP, HALF, HALF, dtype=F32),
    ]
    stats, *saved = call(stats_body, [stat, *tiles, *tiles], [], at, data, other, micros=5)
    stats = swap(stats, ("c1", "c0"))
    half = PART // 2
    dkv, dq, give = call(
        grads_body,
        [
            shape(CHIPS, PART, 2 * D_HEAD),
            shape(CHIPS, half, 2 * D_HEAD),
            shape(CHIPS, PART + half, 2 * D_HEAD),
        ],
        [
            pltpu.VMEM(stat.shape[1:], F32),
            pltpu.VMEM((GROUP, SIDE, 2 * D_HEAD), BF),
            pltpu.VMEM((GROUP, SIDE, 2 * D_HEAD), BF),
            pltpu.VMEM((GROUP, D_HEAD, SIDE), F32),
            pltpu.VMEM((SIDE, 2 * D_HEAD), F32),
        ],
        data, other, stats, *saved,
        micros=7,
    )
    partial = call(
        pair_body, shape(CHIPS, 2 * PART, 2 * D_HEAD), [], at, dkv, dq, meet(give)
    )
    return tuple(call(sum_body, [shape(TOK, wide)] * 3, [], swap(partial, CHIP_AXES)))


def solution(mesh):
    ctx = (*CHIP_AXES, "core")
    split = Mesh(mesh.devices.reshape(4, 2, 2, 2, 2, HEADS), (*ctx, "head"))
    placed = (P(ctx, "head"), P(ctx, "head"), P(ctx, "head"), P((*ctx, "head"), None))
    return jax.shard_map(
        shards,
        mesh=split,
        in_specs=placed,
        out_specs=placed[:3],
        check_vma=False,
    )
```
